128 devices in a mesh: row: 4 (over x), col: 4 (over y_hi, core), shard: 8 (over z, y_lo).
Axes of the slice: x: 4, y: 4 (y_hi: 2, y_lo: 2; y = y_hi * 2 + y_lo), z: 4, core: 2. Of those that a mesh axis runs over, the one named last changes fastest.
Arguments:
- tokens: bfloat16 [4, 4, 2, 1024, 2048], P('row', 'col', None, 'shard'), may hold values from -6 to 6
- cotangent: bfloat16 [4, 4, 2, 1024, 2048], P('row', 'col', None, 'shard'), may hold values from -6 to 6
- w_one: bfloat16 [4, 2048, 7168], P('row', None, 'shard'), may hold values from -6 to 6
- w_two: bfloat16 [4, 7168, 2048], P('col', 'shard'), may hold values from -6 to 6
- late_two: bfloat16 [4, 7168, 2048], P('col', 'shard'), may hold values from -6 to 6
- round_index: int32 [], replicated, may hold values from 0 to 999
Outputs:
- new_one: bfloat16 [4, 2048, 7168], P('row', None, 'shard')
- new_two: bfloat16 [4, 7168, 2048], P('col', 'shard')
- fresh_two: bfloat16 [4, 7168, 2048], P('col', 'shard')
The draws below stay inside these ranges and needn't reach their ends.
All inputs are finite; a program needn't handle non-finite values.
Results may differ from the reference program's by a relative error of at most 0.023.
Values may be sent and summed in bfloat16 or wider, within the bound.
No kernel may reach another device: no remote copies, remote signals or barrier semaphores. Data moves between devices by JAX's collectives and lax.ppermute only.
A program may use at most 512 MiB of HBM per device.

```python
import math
import jax
import jax.numpy as jnp
from jax import lax

D = 2048
FF = 7168
STEPS = 2
GRID_ROWS = 4
GRID_COLS = 4
TOK_PATH = 1024


def shard_levels(key, shape, cuts, least, top_value):
    def one(axis_at, blocks):
        heights = jax.random.uniform(jax.random.fold_in(jax.random.fold_in(key, 6), axis_at), (blocks,), jnp.float32, least / len(cuts), top_value / len(cuts))
        return jnp.repeat(jnp.exp(heights), shape[axis_at] // blocks).reshape((-1,) + (1,) * (len(shape) - axis_at - 1))

    gain = one(*cuts[0])
    for cut in cuts[1:]:
        gain = gain * one(*cut)
    return gain


def bell_draw(own_key, shape, scale, bound, shards=(), dtype=jnp.bfloat16):
    loudness = shard_levels(own_key, shape, shards, -0.22, 0.18) if shards else 1.0
    array = jax.random.normal(own_key, shape, jnp.float32) * scale * loudness
    return jnp.minimum(jnp.maximum(array, -bound), bound).astype(dtype)


def setup_inputs(seed: int = 0) -> dict:
    seeds = jax.random.split(jax.random.key(seed), 7)
    tokens = bell_draw(seeds[0], (GRID_ROWS, GRID_COLS, STEPS, TOK_PATH, D), 1.0, 6.0, ((0, 4), (1, 4), (3, 8)))
    cotangent = bell_draw(seeds[1], (GRID_ROWS, GRID_COLS, STEPS, TOK_PATH, D), 1.0, 6.0, ((0, 4), (1, 4), (3, 8)))
    w_one = bell_draw(seeds[2], (GRID_ROWS, D, FF), 1.0, 6.0, ((0, 4), (2, 8)))
    w_two = bell_draw(seeds[3], (GRID_COLS, FF, D), 1.0, 6.0, ((0, 4), (1, 8)))
    late_two = bell_draw(seeds[4], (GRID_COLS, FF, D), 1.0, 6.0, ((0, 4), (1, 8)))
    round_index = jax.random.randint(seeds[5], (), 0, 1000).astype(jnp.int32)
    return dict(tokens=tokens, cotangent=cotangent, w_one=w_one, w_two=w_two, late_two=late_two, round_index=round_index)


inner_rate = 64.0
warm_rounds = 1000

def rms_rows(tokens):
    values = tokens.astype(jnp.float32)
    scale = lax.rsqrt(lax.optimization_barrier(jnp.mean(values * values, axis=-1, keepdims=True)) + 1e-05)
    return (values * scale).astype(jnp.bfloat16)

def path_grads(tokens, cotangent, first_b, second_b):
    normed = rms_rows(tokens)
    pre_act = jnp.dot(normed, first_b, preferred_element_type=jnp.float32) * D ** (-0.5)
    gates = jax.nn.sigmoid(pre_act)
    active = (pre_act * gates).astype(jnp.bfloat16)
    back_hidden = jnp.dot(cotangent, second_b.T, preferred_element_type=jnp.float32) * FF ** (-0.5)
    pre_grad = (back_hidden * gates * (1.0 + pre_act * (1.0 - gates))).astype(jnp.bfloat16)
    grad_first = jnp.dot(normed.T, pre_grad, preferred_element_type=jnp.float32) * D ** (-0.5)
    grad_second = jnp.dot(active.T, cotangent, preferred_element_type=jnp.float32) * FF ** (-0.5)
    return (grad_first, grad_second)

def reference(tokens, cotangent, w_one, w_two, late_two, round_index):
    step_rate = inner_rate / math.sqrt(TOK_PATH)
    outer_rate = 0.7 * jnp.minimum(round_index + 1, warm_rounds).astype(jnp.float32) / float(warm_rounds)
    sums_one = [jnp.zeros((D, FF), jnp.float32) for row_index in range(GRID_ROWS)]
    sums_two = [jnp.zeros((FF, D), jnp.float32) for col_index in range(GRID_COLS)]
    for row_index in range(GRID_ROWS):
        for col_index in range(GRID_COLS):
            start_one = w_one[row_index].astype(jnp.float32)
            start_two = w_two[col_index].astype(jnp.float32)
            first_weights, second_weights = (start_one, start_two)
            for inner_step in range(STEPS):
                grad_first, grad_second = path_grads(tokens[row_index, col_index, inner_step], cotangent[row_index, col_index, inner_step], first_weights.astype(jnp.bfloat16), second_weights.astype(jnp.bfloat16))
                first_weights = first_weights - step_rate * grad_first
                second_weights = second_weights - step_rate * grad_second
            delta_one = (start_one - first_weights).astype(jnp.bfloat16)
            delta_two = (start_two - second_weights).astype(jnp.bfloat16)
            sums_one[row_index] = sums_one[row_index] + delta_one.astype(jnp.float32)
            sums_two[col_index] = sums_two[col_index] + delta_two.astype(jnp.float32)
    new_one = jnp.stack([(w_one[row_index].astype(jnp.float32) - outer_rate * sums_one[row_index] / GRID_COLS).astype(jnp.bfloat16) for row_index in range(GRID_ROWS)])
    new_two = (w_two.astype(jnp.float32) - outer_rate * late_two.astype(jnp.float32)).astype(jnp.bfloat16)
    fresh_two = jnp.stack([(sums_two[col_index] / GRID_ROWS).astype(jnp.bfloat16) for col_index in range(GRID_COLS)])
    return (new_one, new_two, fresh_two)
```

```python
import math

import jax
import jax.numpy as jnp
from jax import lax
from jax.sharding import PartitionSpec as P

D = 2048
FF = 7168


inner_rate = 64.0
warm_rounds = 1000

Z = 4


def along_z(hop):
    return [(z * 2 + y, ((z + hop) % Z) * 2 + y) for z in range(Z) for y in range(2)]


across_y = [(z * 2 + y, z * 2 + 1 - y) for z in range(Z) for y in range(2)]
across_core = [(h * 2 + k, h * 2 + 1 - k) for h in range(2) for k in range(2)]
across_half = [(h * 2 + k, (1 - h) * 2 + k) for h in range(2) for k in range(2)]
even_pairs = [(0, 1), (1, 0), (2, 3), (3, 2)]
odd_pairs = [(1, 2), (2, 1), (3, 0), (0, 3)]


def up(block):
    return lax.ppermute(block, "shard", along_z(1))


def down(block):
    return lax.ppermute(block, "shard", along_z(-1))


def side(block):
    return lax.ppermute(block, "shard", across_y)


def spread(own, plan):
    below = up(own)
    above = down(own)
    beside = side(own)
    if plan == "side":
        beside_below = side(below)
        beside_above = side(above)
        far = up(below)
        beside_far = down(beside_above)
    else:
        beside_below = up(beside)
        beside_above = down(beside)
        if plan == "up":
            far = up(below)
            beside_far = side(far)
        elif plan == "down":
            far = down(above)
            beside_far = side(far)
        else:
            half = own.shape[0] // 2
            far_low = up(below[:half])
            far_high = down(above[half:])
            far = jnp.concatenate([far_low, far_high])
            beside_far = jnp.concatenate([side(far_low), side(far_high)])
    near = jnp.concatenate([own, below, above, beside])
    rest = jnp.concatenate([beside_below, beside_above, far, beside_far])
    return near, rest


def rms_rows(tokens):
    values = tokens.astype(jnp.float32)
    scale = lax.rsqrt(jnp.mean(values * values, axis=-1, keepdims=True) + 1e-05)
    return (values * scale).astype(jnp.bfloat16)


def hidden_parts(normed, cotangent, first_b, second_b):
    pre_act = jnp.dot(normed, first_b, preferred_element_type=jnp.float32) * D ** (-0.5)
    gates = jax.nn.sigmoid(pre_act)
    active = (pre_act * gates).astype(jnp.bfloat16)
    back_hidden = jnp.dot(cotangent, second_b.T, preferred_element_type=jnp.float32) * FF ** (-0.5)
    pre_grad = (back_hidden * gates * (1.0 + pre_act * (1.0 - gates))).astype(jnp.bfloat16)
    return (active, pre_grad)


def add(left, right):
    return (left.astype(jnp.float32) + right.astype(jnp.float32)).astype(jnp.bfloat16)


def halves(block, bit):
    size = block.shape[0] // 2
    kept = lax.dynamic_slice_in_dim(block, bit * size, size)
    sent = lax.dynamic_slice_in_dim(block, (1 - bit) * size, size)
    return kept, sent


def join(kept, other, bit):
    return jnp.where(
        bit == 0, jnp.concatenate([kept, other]), jnp.concatenate([other, kept])
    )


def sum_ring(block, first, second, first_bit, second_bit):
    kept, sent = halves(block, first_bit)
    total = add(kept, lax.ppermute(sent, "row", first))
    kept, sent = halves(total, second_bit)
    total = add(kept, lax.ppermute(sent, "row", second))
    total = join(total, lax.ppermute(total, "row", second), second_bit)
    return join(total, lax.ppermute(total, "row", first), first_bit)


def sum_col(block, bit):
    kept, sent = halves(block, bit)
    total = add(kept, lax.ppermute(sent, "col", across_core))
    total = add(total, lax.ppermute(total, "col", across_half))
    return join(total, lax.ppermute(total, "col", across_core), bit)


def shards(tokens, cotangent, w_one, w_two, late_two, round_index):
    first_b = w_one[0]
    second_b = w_two[0]
    path_rows = tokens.shape[3] * lax.axis_size("shard")
    step_rate = inner_rate / math.sqrt(path_rows)
    row = lax.axis_index("row")
    low_bit = ((row + 1) // 2) % 2
    high_bit = row // 2
    core_bit = lax.axis_index("col") % 2

    plans = (("up", "down"), ("side", "split"))
    steps = tokens.shape[2]
    gathered = []
    for inner_step in range(steps):
        token_plan, cot_plan = plans[inner_step % 2]
        gathered.append(
            (
                spread(tokens[0, 0, inner_step], token_plan),
                spread(cotangent[0, 0, inner_step], cot_plan),
            )
        )
    cur_first, cur_second = first_b, second_b
    step_one = jnp.zeros(first_b.shape, jnp.float32)
    step_two = jnp.zeros(second_b.shape, jnp.float32)
    for inner_step in range(steps):
        token_parts, cot_parts = gathered[inner_step]
        normed = [rms_rows(part) for part in token_parts]
        parts = [
            hidden_parts(n, g, cur_first, cur_second) for n, g in zip(normed, cot_parts)
        ]
        normed = jnp.concatenate(normed)
        cots = jnp.concatenate(cot_parts)
        active = jnp.concatenate([p[0] for p in parts])
        pre_grad = jnp.concatenate([p[1] for p in parts])
        grad_two = jnp.dot(active.T, cots, preferred_element_type=jnp.float32) * FF ** (-0.5)
        grad_one = jnp.dot(normed.T, pre_grad, preferred_element_type=jnp.float32) * D ** (-0.5)
        step_one = step_one + step_rate * grad_one
        step_two = step_two + step_rate * grad_two
        if inner_step + 1 < steps:
            cur_first = (first_b.astype(jnp.float32) - step_one).astype(jnp.bfloat16)
            cur_second = (second_b.astype(jnp.float32) - step_two).astype(jnp.bfloat16)
    delta_one = step_one.astype(jnp.bfloat16)
    delta_two = step_two.astype(jnp.bfloat16)

    half = delta_two.shape[0] // 2
    sum_two = jnp.concatenate(
        [
            sum_ring(delta_two[:half], even_pairs, odd_pairs, low_bit, high_bit),
            sum_ring(delta_two[half:], odd_pairs, even_pairs, high_bit, low_bit),
        ]
    )
    sum_one = sum_col(delta_one, core_bit)

    outer_rate = (
        0.7 * jnp.minimum(round_index + 1, warm_rounds).astype(jnp.float32) / float(warm_rounds)
    )
    mean_one = sum_one.astype(jnp.float32) / lax.axis_size("col")
    new_one = (first_b.astype(jnp.float32) - outer_rate * mean_one).astype(jnp.bfloat16)
    fresh_two = (sum_two.astype(jnp.float32) / lax.axis_size("row")).astype(jnp.bfloat16)
    new_two = (second_b.astype(jnp.float32) - outer_rate * late_two[0].astype(jnp.float32)).astype(
        jnp.bfloat16
    )
    return (new_one[None], new_two[None], fresh_two[None])


def solution(mesh):
    in_specs = (
        P("row", "col", None, "shard", None),
        P("row", "col", None, "shard", None),
        P("row", None, "shard"),
        P("col", "shard", None),
        P("col", "shard", None),
        P(),
    )
    out_specs = (P("row", None, "shard"), P("col", "shard", None), P("col", "shard", None))
    return jax.shard_map(shards, mesh=mesh, in_specs=in_specs, out_specs=out_specs, check_vma=False)
```

```python
import math

import jax
import jax.numpy as jnp
from jax import lax
from jax.sharding import PartitionSpec as P

D = 2048
FF = 7168


inner_rate = 64.0
warm_rounds = 1000

Z = 4


def along_z(hop):
    return [(z * 2 + y, ((z + hop) % Z) * 2 + y) for z in range(Z) for y in range(2)]


across_y = [(z * 2 + y, z * 2 + 1 - y) for z in range(Z) for y in range(2)]
across_core = [(h * 2 + k, h * 2 + 1 - k) for h in range(2) for k in range(2)]
across_half = [(h * 2 + k, (1 - h) * 2 + k) for h in range(2) for k in range(2)]
even_pairs = [(0, 1), (1, 0), (2, 3), (3, 2)]
odd_pairs = [(1, 2), (2, 1), (3, 0), (0, 3)]

moves = {"up": along_z(1), "down": along_z(-1), "side": across_y}

rounds = [
    [("x0b", "up", "x0o"), ("x0a", "down", "x0o"), ("x0s", "side", "x0o")],
    [("g0b", "up", "g0o"), ("g0a", "down", "g0o"), ("g0s", "side", "g0o")],
    [("x0f", "up", "x0b"), ("x0sa", "down", "x0s"), ("x0sb", "side", "x0b")],
    [("g0f", "up", "g0b"), ("g0sa", "down", "g0s"), ("g0sb", "side", "g0b")],
    [("x1b", "up", "x1o"), ("x1a", "down", "x1o"), ("x0sf", "side", "x0f")],
    [("g1b", "up", "g1o"), ("g1a", "down", "g1o"), ("g0sf", "side", "g0f")],
    [("x1f", "up", "x1b"), ("x1s", "side", "x1o")],
    [("g1f", "down", "g1a"), ("g1s", "side", "g1o")],
    [("x1sb", "up", "x1s"), ("x1sa", "down", "x1s"), ("x1sf", "side", "x1f")],
    [("g1sb", "up", "g1s"), ("g1sa", "down", "g1s"), ("g1sf", "side", "g1f")],
]


def tie(state, names):
    names = sorted(set(names))
    state.update(zip(names, lax.optimization_barrier(tuple(state[n] for n in names))))


def rms_rows(tokens):
    values = tokens.astype(jnp.float32)
    scale = lax.rsqrt(jnp.mean(values * values, axis=-1, keepdims=True) + 1e-05)
    return (values * scale).astype(jnp.bfloat16)


def hidden_parts(normed, cotangent, first_b, second_b):
    pre_act = jnp.dot(normed, first_b, preferred_element_type=jnp.float32) * D ** (-0.5)
    gates = jax.nn.sigmoid(pre_act)
    active = (pre_act * gates).astype(jnp.bfloat16)
    back_hidden = jnp.dot(cotangent, second_b.T, preferred_element_type=jnp.float32) * FF ** (-0.5)
    pre_grad = (back_hidden * gates * (1.0 + pre_act * (1.0 - gates))).astype(jnp.bfloat16)
    return (active, pre_grad)


def add(left, right):
    return (left.astype(jnp.float32) + right.astype(jnp.float32)).astype(jnp.bfloat16)


def halves(block, bit, axis=0):
    size = block.shape[axis] // 2
    kept = lax.dynamic_slice_in_dim(block, bit * size, size, axis)
    sent = lax.dynamic_slice_in_dim(block, (1 - bit) * size, size, axis)
    return kept, sent


def place(whole, block, bit, start=0):
    return lax.dynamic_update_slice_in_dim(whole, block, start + bit * block.shape[0], 0)


def shards(tokens, cotangent, w_one, w_two, late_two, round_index):
    first_b = w_one[0]
    second_b = w_two[0]
    path_rows = tokens.shape[3] * lax.axis_size("shard")
    step_rate = inner_rate / math.sqrt(path_rows)
    row = lax.axis_index("row")
    low_bit = ((row + 1) // 2) % 2
    high_bit = row // 2
    core_bit = lax.axis_index("col") % 2
    cols = lax.axis_size("col")
    rows = lax.axis_size("row")
    outer_rate = (
        0.7 * jnp.minimum(round_index + 1, warm_rounds).astype(jnp.float32) / float(warm_rounds)
    )

    state = {}
    for step in range(2):
        state["x%do" % step] = tokens[0, 0, step]
        state["g%do" % step] = cotangent[0, 0, step]
    state["w1"], state["w2"] = first_b, second_b

    def normed(step, ends, tag):
        state["n" + tag] = rms_rows(jnp.concatenate([state["x%d%s" % (step, e)] for e in ends]))

    def cots(step, ends, tag):
        state["g" + tag] = jnp.concatenate([state["g%d%s" % (step, e)] for e in ends])

    def ahead(tag):
        pre_act = jnp.dot(state["n" + tag], state["w1"], preferred_element_type=jnp.float32) * D ** (
            -0.5
        )
        gates = jax.nn.sigmoid(pre_act)
        state["u" + tag] = (pre_act * gates).astype(jnp.bfloat16)
        state["p" + tag] = gates * (1.0 + pre_act * (1.0 - gates))

    def back(tag):
        back_hidden = jnp.dot(
            state["g" + tag], state["w2"].T, preferred_element_type=jnp.float32
        ) * FF ** (-0.5)
        state["q" + tag] = (back_hidden * state["p" + tag]).astype(jnp.bfloat16)

    def grad_one(tags):
        n, q = [jnp.concatenate([state[k + t] for t in tags]) for k in "nq"]
        grad = jnp.dot(n.T, q, preferred_element_type=jnp.float32) * D ** (-0.5)
        return step_rate * grad

    def grad_two(tags, columns=slice(None)):
        u, g = [jnp.concatenate([state[k + t] for t in tags]) for k in "ug"]
        grad = jnp.dot(u.T, g[:, columns], preferred_element_type=jnp.float32) * FF ** (-0.5)
        return step_rate * grad

    near, rest = ("o", "b", "a", "s"), ("sb", "sa", "f", "sf")
    for k, transfers in enumerate(rounds):
        for made, way, sent in transfers:
            state[made] = lax.ppermute(state[sent], "shard", moves[way])
        done = []
        if k == 3:
            normed(0, near, "0n"), cots(0, near, "0n"), ahead("0n"), back("0n")
            done += ["n0n", "g0n", "u0n", "q0n"]
        if k == 6:
            normed(0, rest, "0r"), cots(0, rest, "0r"), ahead("0r"), back("0r")
            done += ["n0r", "g0r", "u0r", "q0r"]
        if k == 7:
            step_one, step_two = grad_one(("0n", "0r")), grad_two(("0n", "0r"))
            state["w1"] = (first_b.astype(jnp.float32) - step_one).astype(jnp.bfloat16)
            state["w2"] = (second_b.astype(jnp.float32) - step_two).astype(jnp.bfloat16)
            state["d1"], state["d2"] = step_one.astype(jnp.bfloat16), step_two.astype(jnp.bfloat16)
            done += ["d1", "d2", "w1", "w2"]
        if k == 8:
            normed(1, near, "1n"), cots(1, near, "1n"), ahead("1n"), back("1n")
            done += ["n1n", "g1n", "u1n", "q1n"]
        if k == 9:
            state["d1"] = (state["d1"].astype(jnp.float32) + grad_one(("1n",))).astype(jnp.bfloat16)
            state["d2"] = (state["d2"].astype(jnp.float32) + grad_two(("1n",))).astype(jnp.bfloat16)
            normed(1, rest, "1r"), ahead("1r")
            done += ["d1", "d2", "n1r", "u1r", "p1r"]
        later = [t[2] for t in (rounds[k + 2] if k + 2 < len(rounds) else [])]
        tie(state, [t[0] for t in transfers] + later + done)

    cots(1, rest, "1r")
    half = second_b.shape[0] // 2
    width = second_b.shape[1] // 2
    ways = {"a": (even_pairs, odd_pairs, low_bit, high_bit), "b": (odd_pairs, even_pairs, high_bit, low_bit)}
    for c in "01":
        columns = slice(int(c) * width, (int(c) + 1) * width)
        delta = state["d2"][:, columns].astype(jnp.float32) + grad_two(("1r",), columns)
        delta = delta.astype(jnp.bfloat16)
        for p, (first, second, first_bit, second_bit) in ways.items():
            state["k" + p + c], state["s" + p + c] = halves(
                delta[:half] if p == "a" else delta[half:], first_bit
            )
            state["r" + p + c] = lax.ppermute(state["s" + p + c], "row", first)
        if c == "0":
            tie(state, ["d2", "g1r", "u1r", "sa0", "sb0"])
    tie(state, ["sa1", "sb1", "g1r", "p1r"])
    back("1r")
    tie(state, ["ra0", "rb0", "q1r", "d1", "n1r", "ka0", "kb0"])

    def second_stage(c):
        for p, (first, second, first_bit, second_bit) in ways.items():
            state["k" + p + c], state["s" + p + c] = halves(
                add(state["k" + p + c], state["r" + p + c]), second_bit
            )

    def send_second(c):
        for p, (first, second, first_bit, second_bit) in ways.items():
            state["r" + p + c] = lax.ppermute(state["s" + p + c], "row", second)

    def third_stage(c):
        for p, (first, second, first_bit, second_bit) in ways.items():
            total = state["k" + p + c].astype(jnp.float32) + state["r" + p + c].astype(jnp.float32)
            state["t" + p + c] = (total / rows).astype(jnp.bfloat16)

    def send_third(c):
        for p, (first, second, first_bit, second_bit) in ways.items():
            state["r" + p + c] = lax.ppermute(state["t" + p + c], "row", second)

    def fourth_stage(c):
        for p, (first, second, first_bit, second_bit) in ways.items():
            mine, theirs = state["t" + p + c], state["r" + p + c]
            whole = jnp.zeros((2 * mine.shape[0], mine.shape[1]), mine.dtype)
            state["t" + p + c] = place(place(whole, mine, second_bit), theirs, 1 - second_bit)

    def send_fourth(c):
        for p, (first, second, first_bit, second_bit) in ways.items():
            state["r" + p + c] = lax.ppermute(state["t" + p + c], "row", first)

    second_stage("0")
    tie(state, ["sa0", "sb0", "q1r", "d1", "n1r"])
    send_second("0")
    delta = (state["d1"].astype(jnp.float32) + grad_one(("1r",))).astype(jnp.bfloat16)
    state["k1"], state["s1"] = halves(delta, core_bit)
    state["r1"] = lax.ppermute(state["s1"], "col", across_core)
    tie(state, ["ra1", "rb1", "s1", "k1", "ka1", "kb1"])
    second_stage("1")
    tie(state, ["sa1", "sb1", "ra0", "rb0", "ka0", "kb0"])
    send_second("1")
    third_stage("0")
    tie(state, ["r1", "k1", "ta0", "tb0"])
    send_third("0")
    state["t1"] = add(state["k1"], state["r1"])
    tie(state, ["t1", "ra1", "rb1", "ka1", "kb1"])
    state["r1"] = lax.ppermute(state["t1"], "col", across_half)
    third_stage("1")
    tie(state, ["ra0", "rb0", "ta0", "tb0", "ta1", "tb1"])
    send_third("1")
    fourth_stage("0")
    tie(state, ["ra1", "rb1", "ta1", "tb1", "ta0", "tb0"])
    send_fourth("0")
    fourth_stage("1")
    tie(state, ["ta1", "tb1", "ta0", "tb0", "ra0", "rb0"])
    send_fourth("1")
    tie(state, ["r1", "t1", "ta0", "tb0", "ra0", "rb0"])
    mean_one = (state["t1"].astype(jnp.float32) + state["r1"].astype(jnp.float32)) / cols
    half_rows = first_b.shape[0] // 2
    own_first = lax.dynamic_slice_in_dim(first_b, core_bit * half_rows, half_rows, 0)
    state["t1"] = (own_first.astype(jnp.float32) - outer_rate * mean_one).astype(jnp.bfloat16)
    state["r1"] = lax.ppermute(state["t1"], "col", across_core)

    fresh_two = jnp.zeros(second_b.shape, jnp.bfloat16)
    for c in "01":
        for p, (first, second, first_bit, second_bit) in ways.items():
            start = 0 if p == "a" else half
            mine, theirs = state["t" + p + c], state["r" + p + c]
            size = mine.shape[0]
            fresh_two = lax.dynamic_update_slice(
                fresh_two, mine, (start + first_bit * size, int(c) * width)
            )
            fresh_two = lax.dynamic_update_slice(
                fresh_two, theirs, (start + (1 - first_bit) * size, int(c) * width)
            )
    new_one = place(jnp.zeros(first_b.shape, jnp.bfloat16), state["t1"], core_bit)
    new_one = place(new_one, state["r1"], 1 - core_bit)
    new_two = (second_b.astype(jnp.float32) - outer_rate * late_two[0].astype(jnp.float32)).astype(
        jnp.bfloat16
    )
    return (new_one[None], new_two[None], fresh_two[None])


def solution(mesh):
    in_specs = (
        P("row", "col", None, "shard", None),
        P("row", "col", None, "shard", None),
        P("row", None, "shard"),
        P("col", "shard", None),
        P("col", "shard", None),
        P(),
    )
    out_specs = (P("row", None, "shard"), P("col", "shard", None), P("col", "shard", None))
    return jax.shard_map(shards, mesh=mesh, in_specs=in_specs, out_specs=out_specs, check_vma=False)
```

```python
import functools
import math

import jax
import jax.numpy as jnp
from jax import lax
from jax.experimental import pallas as pl
from jax.experimental.pallas import tpu as pltpu
from jax.sharding import PartitionSpec as P

D = 2048
FF = 7168


inner_rate = 64.0
warm_rounds = 1000

Z = 4


def along_z(hop):
    return [(z * 2 + y, ((z + hop) % Z) * 2 + y) for z in range(Z) for y in range(2)]


across_y = [(z * 2 + y, z * 2 + 1 - y) for z in range(Z) for y in range(2)]
across_core = [(h * 2 + k, h * 2 + 1 - k) for h in range(2) for k in range(2)]
across_half = [(h * 2 + k, (1 - h) * 2 + k) for h in range(2) for k in range(2)]
even_pairs = [(0, 1), (1, 0), (2, 3), (3, 2)]
odd_pairs = [(1, 2), (2, 1), (3, 0), (0, 3)]

moves = {"up": along_z(1), "down": along_z(-1), "side": across_y}


def move(block, way, name):
    with jax.named_scope(name):
        return lax.ppermute(block, "shard", moves[way])


def tie(state, names):
    names = sorted(set(names.split()))
    state.update(zip(names, lax.optimization_barrier(tuple(state[n] for n in names))))


def after(value, *others):
    return lax.optimization_barrier((value,) + others)[0]


def rms_rows(tokens):
    values = tokens.astype(jnp.float32)
    scale = lax.rsqrt(jnp.mean(values * values, axis=-1, keepdims=True) + 1e-05)
    return (values * scale).astype(jnp.bfloat16)


def forward_kernel(count, *refs):
    first, second, normed, cots, active, pre_grad = refs[2 * count :]
    share = refs[0].shape[0]

    @pl.when(pl.program_id(0) == 0)
    def _():
        for i in range(count):
            normed[i * share : (i + 1) * share, :] = rms_rows(refs[2 * i][...])
            cots[i * share : (i + 1) * share, :] = refs[2 * i + 1][...]

    pre_act = jnp.dot(normed[...], first[...], preferred_element_type=jnp.float32) * D ** (-0.5)
    gates = jax.nn.sigmoid(pre_act)
    active[...] = (pre_act * gates).astype(jnp.bfloat16)
    back_hidden = lax.dot_general(
        cots[...], second[...], (((1,), (1,)), ((), ())), preferred_element_type=jnp.float32
    ) * FF ** (-0.5)
    pre_grad[...] = (back_hidden * gates * (1.0 + pre_act * (1.0 - gates))).astype(jnp.bfloat16)


def forward(pairs, first_b, second_b):
    tile = 256
    width, hidden = first_b.shape
    share = pairs[0][0][0].shape[0]
    total = share * len(pairs)

    def side_spec(part):
        return pl.BlockSpec((share, width), lambda j: (0, part))

    operands, specs = [], []
    for pair in pairs:
        for array, part in pair:
            operands.append(array)
            specs.append(side_spec(part))
    whole = jax.ShapeDtypeStruct((total, width), jnp.bfloat16)
    narrow = jax.ShapeDtypeStruct((total, hidden), jnp.bfloat16)
    return pl.pallas_call(
        functools.partial(forward_kernel, len(pairs)),
        grid=(pl.cdiv(hidden, tile),),
        in_specs=specs
        + [
            pl.BlockSpec((width, tile), lambda j: (0, j)),
            pl.BlockSpec((tile, width), lambda j: (j, 0)),
        ],
        out_specs=[pl.BlockSpec((total, width), lambda j: (0, 0))] * 2
        + [pl.BlockSpec((total, tile), lambda j: (0, j))] * 2,
        out_shape=[whole, whole, narrow, narrow],
        compiler_params=pltpu.CompilerParams(vmem_limit_bytes=32 * 1024 * 1024),
        cost_estimate=pl.CostEstimate(
            flops=4 * total * width * hidden,
            bytes_accessed=4 * width * hidden + 8 * total * width + 4 * total * hidden,
            transcendentals=total * hidden,
        ),
    )(*operands, first_b, second_b)


def add(left, right):
    return (left.astype(jnp.float32) + right.astype(jnp.float32)).astype(jnp.bfloat16)


def halves(block, bit, axis=0):
    size = block.shape[axis] // 2
    kept = lax.dynamic_slice_in_dim(block, bit * size, size, axis)
    sent = lax.dynamic_slice_in_dim(block, (1 - bit) * size, size, axis)
    return kept, sent


def place(whole, block, bit, start=0):
    return lax.dynamic_update_slice_in_dim(whole, block, start + bit * block.shape[0], 0)


def shards(tokens, cotangent, w_one, w_two, late_two, round_index):
    first_b = w_one[0]
    second_b = w_two[0]
    path_rows = tokens.shape[3] * lax.axis_size("shard")
    step_rate = inner_rate / math.sqrt(path_rows)
    row = lax.axis_index("row")
    low_bit = ((row + 1) // 2) % 2
    high_bit = row // 2
    core_bit = lax.axis_index("col") % 2
    cols = lax.axis_size("col")
    rows = lax.axis_size("row")
    outer_rate = (
        0.7 * jnp.minimum(round_index + 1, warm_rounds).astype(jnp.float32) / float(warm_rounds)
    )

    state = {}
    for step in range(2):
        state["%do" % step] = jnp.concatenate([tokens[0, 0, step], cotangent[0, 0, step]], axis=1)
    width = tokens.shape[4]
    state["w1"], state["w2"] = first_b, second_b

    def rest_of_block(tag, kind):
        return state[tag][:, :width] if kind == "x" else state[tag][:, width:]

    def ahead(step, ends, tag):
        blocks = [state[str(step) + e] for e in ends.split()]
        pairs = [((e, 0), (e, 1)) for e in blocks]
        values = forward(pairs, state["w1"], state["w2"])
        state.update(zip(("n" + tag, "g" + tag, "u" + tag, "q" + tag), values))

    def ahead_last(step, tag):
        pairs = [((state["%dex" % step], 0), (state["%deg" % step], 0))]
        values = forward(pairs, state["w1"], state["w2"])
        state.update(zip(("n" + tag, "g" + tag, "u" + tag, "q" + tag), values))

    def grad_one(tags):
        n, q = [jnp.concatenate([state[k + t] for t in tags.split()]) for k in "nq"]
        grad = jnp.dot(n.T, q, preferred_element_type=jnp.float32) * D ** (-0.5)
        return step_rate * grad

    def grad_two(tags):
        u, g = [jnp.concatenate([state[k + t] for t in tags.split()]) for k in "ug"]
        grad = jnp.dot(u.T, g, preferred_element_type=jnp.float32) * FF ** (-0.5)
        return step_rate * grad

    def grow(name, grad):
        state[name] = (state[name].astype(jnp.float32) + grad).astype(jnp.bfloat16)

    def first_moves(step):
        own = "%do" % step
        for end, way in (("b", "up"), ("a", "down"), ("s", "side")):
            state[str(step) + end] = move(state[own], way, "gather_%d%s" % (step, end))

    def second_moves(step):
        for end, sent, way in (("f", "b", "up"), ("c", "s", "down"), ("d", "b", "side")):
            state[str(step) + end] = move(
                state[str(step) + sent], way, "gather_%d%s" % (step, end)
            )

    def last_moves(step):
        low = move(rest_of_block("%dd" % step, "x"), "up", "gather_%dex" % step)
        high = move(rest_of_block("%dc" % step, "g"), "down", "gather_%deg" % step)
        state["%dex" % step], state["%deg" % step] = low, high

    first_moves(0)
    state["new"] = (
        second_b.astype(jnp.float32) - outer_rate * late_two[0].astype(jnp.float32)
    ).astype(jnp.bfloat16)
    tie(state, "0b 0a 0s 0o 1o new")
    second_moves(0)
    ahead(0, "o b a s", "0n")
    state["1o"] = after(state["1o"], state["q0n"])
    state["1b"] = move(state["1o"], "up", "gather_1b")
    state["1a"] = move(state["1o"], "down", "gather_1a")
    state["d1"] = grad_one("0n").astype(jnp.bfloat16)
    state["d2"] = grad_two("0n").astype(jnp.bfloat16)
    tie(state, "0f 0c 0d n0n g0n u0n q0n d1 d2 1o")
    last_moves(0)
    state["1s"] = move(state["1o"], "side", "gather_1s")
    ahead(0, "f c d", "0m")
    tie(state, "1b 1a 1s d1 d2 n0m g0m u0m q0m w1 w2")
    second_moves(1)
    ahead_last(0, "0l")
    grow("d1", grad_one("0m 0l")), grow("d2", grad_two("0m 0l"))
    tie(state, "d1 d2")
    state["w1"] = (first_b.astype(jnp.float32) - state["d1"].astype(jnp.float32)).astype(jnp.bfloat16)
    state["w2"] = (second_b.astype(jnp.float32) - state["d2"].astype(jnp.float32)).astype(jnp.bfloat16)
    tie(state, "d1 d2 w1 w2")
    ahead(1, "o b a s", "1n")
    tie(state, "1f 1c 1d n1n g1n u1n q1n d1 d2")
    last_moves(1)
    grow("d1", grad_one("1n")), grow("d2", grad_two("1n"))
    ahead(1, "f c d", "1m")
    tie(state, "1ex 1eg n1m g1m u1m q1m d1 d2")
    ahead_last(1, "1l")

    def part(array, bit, parts, axis):
        size = array.shape[axis] // parts
        return lax.dynamic_slice_in_dim(array, bit * size, size, axis)

    def delta_one(bit):
        n, q = [jnp.concatenate([state[k + t] for t in ("1m", "1l")]) for k in "nq"]
        n = part(n, bit, 2, 1)
        grad = jnp.dot(n.T, q, preferred_element_type=jnp.float32) * D ** (-0.5)
        old = part(state["d1"], bit, 2, 0).astype(jnp.float32)
        return (old + step_rate * grad).astype(jnp.bfloat16)

    def delta_two(quarter):
        u, g = [jnp.concatenate([state[k + t] for t in ("1m", "1l")]) for k in "ug"]
        g = part(g, quarter, 4, 1)
        grad = jnp.dot(u.T, g, preferred_element_type=jnp.float32) * FF ** (-0.5)
        old = part(state["d2"], quarter, 4, 1).astype(jnp.float32)
        return (old + step_rate * grad).astype(jnp.bfloat16)

    ways = {
        "a": (even_pairs, odd_pairs, low_bit, high_bit, 0),
        "b": (odd_pairs, even_pairs, high_bit, low_bit, 2),
    }

    def trade(block, pairs, name):
        with jax.named_scope(name):
            return lax.ppermute(block, "row", pairs)

    state["s1"] = delta_one(1 - core_bit)
    with jax.named_scope("col_1"):
        other_one = lax.ppermute(state["s1"], "col", across_core)
    tie(state, "s1 u1m u1l g1m g1l d2")
    got, kept = {}, {}
    for p, (first, second, first_bit, second_bit, start) in ways.items():
        state["s" + p] = delta_two(start + 1 - first_bit)
        got[p] = trade(state["s" + p], first, "row_1" + p)
    tie(state, "sa sb n1m n1l q1m q1l d1 u1m u1l g1m g1l d2")
    total_one = add(delta_one(core_bit), other_one)
    with jax.named_scope("col_2"):
        other_one = lax.ppermute(total_one, "col", across_half)
    for p, (first, second, first_bit, second_bit, start) in ways.items():
        kept[p] = delta_two(start + first_bit)

    rows_two = second_b.shape[0]
    half = rows_two // 2
    fresh = {}
    for c in range(2):
        chunk = slice(c * half, (c + 1) * half)
        for p, (first, second, first_bit, second_bit, start) in ways.items():
            total = add(kept[p][chunk], after(got[p], total_one)[chunk])
            keep, sent = halves(total, second_bit, 1)
            other = trade(sent, second, "row_2%s%d" % (p, c))
            total = keep.astype(jnp.float32) + other.astype(jnp.float32)
            mine = (total / rows).astype(jnp.bfloat16)
            theirs = trade(mine, second, "row_3%s%d" % (p, c))
            size = mine.shape[1]
            mine, theirs = [
                jnp.where(second_bit == 0, l, r) for l, r in ((mine, theirs), (theirs, mine))
            ]
            mine = jnp.concatenate([mine, theirs], axis=1)
            fresh[p, c] = mine, trade(mine, first, "row_4%s%d" % (p, c))

    last = fresh["b", 1][0]
    mean_one = (
        total_one.astype(jnp.float32) + after(other_one, last).astype(jnp.float32)
    ) / cols
    half_rows = first_b.shape[0] // 2
    own_first = lax.dynamic_slice_in_dim(first_b, core_bit * half_rows, half_rows, 0)
    mine_one = (own_first.astype(jnp.float32) - outer_rate * mean_one).astype(jnp.bfloat16)
    with jax.named_scope("col_3"):
        theirs_one = lax.ppermute(mine_one, "col", across_core)

    new_one = place(jnp.zeros(first_b.shape, jnp.bfloat16), mine_one, core_bit)
    new_one = place(new_one, theirs_one, 1 - core_bit)
    fresh_two = jnp.zeros(second_b.shape, jnp.bfloat16)
    for (p, c), (mine, theirs) in fresh.items():
        first_bit, start, size = ways[p][2], ways[p][4], mine.shape[1]
        if (p, c) == ("b", 1):
            theirs, new_one = lax.optimization_barrier((theirs, new_one))
        fresh_two = lax.dynamic_update_slice(
            fresh_two, mine, (c * half, (start + first_bit) * size)
        )
        fresh_two = lax.dynamic_update_slice(
            fresh_two, theirs, (c * half, (start + 1 - first_bit) * size)
        )
    return (new_one[None], state["new"][None], fresh_two[None])


def solution(mesh):
    in_specs = (
        P("row", "col", None, "shard", None),
        P("row", "col", None, "shard", None),
        P("row", None, "shard"),
        P("col", "shard", None),
        P("col", "shard", None),
        P(),
    )
    out_specs = (P("row", None, "shard"), P("col", "shard", None), P("col", "shard", None))
    return jax.shard_map(shards, mesh=mesh, in_specs=in_specs, out_specs=out_specs, check_vma=False)
```

```python
import functools
import math

import jax
import jax.numpy as jnp
from jax import lax
from jax.experimental import pallas as pl
from jax.experimental.pallas import tpu as pltpu
from jax.sharding import PartitionSpec as P

D = 2048
FF = 7168


inner_rate = 64.0
warm_rounds = 1000

Z = 4


def along_z(hop):
    return [(z * 2 + y, ((z + hop) % Z) * 2 + y) for z in range(Z) for y in range(2)]


across_y = [(z * 2 + y, z * 2 + 1 - y) for z in range(Z) for y in range(2)]
across_core = [(h * 2 + k, h * 2 + 1 - k) for h in range(2) for k in range(2)]
across_half = [(h * 2 + k, (1 - h) * 2 + k) for h in range(2) for k in range(2)]
even_pairs = [(0, 1), (1, 0), (2, 3), (3, 2)]
odd_pairs = [(1, 2), (2, 1), (3, 0), (0, 3)]

moves = {"up": along_z(1), "down": along_z(-1), "side": across_y}


def move(block, way, name):
    with jax.named_scope(name):
        return lax.ppermute(block, "shard", moves[way])


def tie(state, names):
    names = sorted(set(names.split()))
    state.update(zip(names, lax.optimization_barrier(tuple(state[n] for n in names))))


def after(value, *others):
    return lax.optimization_barrier((value,) + others)[0]


def rms_rows(tokens):
    values = tokens.astype(jnp.float32)
    scale = lax.rsqrt(jnp.mean(values * values, axis=-1, keepdims=True) + 1e-05)
    return (values * scale).astype(jnp.bfloat16)


def forward_kernel(count, *refs):
    first, second, normed, cots, active, pre_grad = refs[2 * count :]
    share = refs[0].shape[0]

    @pl.when(pl.program_id(0) == 0)
    def _():
        for i in range(count):
            normed[i * share : (i + 1) * share, :] = rms_rows(refs[2 * i][...])
            cots[i * share : (i + 1) * share, :] = refs[2 * i + 1][...]

    pre_act = jnp.dot(normed[...], first[...], preferred_element_type=jnp.float32) * D ** (-0.5)
    gates = jax.nn.sigmoid(pre_act)
    active[...] = (pre_act * gates).astype(jnp.bfloat16)
    back_hidden = lax.dot_general(
        cots[...], second[...], (((1,), (1,)), ((), ())), preferred_element_type=jnp.float32
    ) * FF ** (-0.5)
    pre_grad[...] = (back_hidden * gates * (1.0 + pre_act * (1.0 - gates))).astype(jnp.bfloat16)


def forward(pairs, first_b, second_b):
    tile = 256
    once = pl.Buffered(1)
    width, hidden = first_b.shape
    share = pairs[0][0][0].shape[0]
    total = share * len(pairs)

    def side_spec(part):
        return pl.BlockSpec((share, width), lambda j: (0, part), pipeline_mode=once)

    operands, specs = [], []
    for pair in pairs:
        for array, part in pair:
            operands.append(array)
            specs.append(side_spec(part))
    whole = jax.ShapeDtypeStruct((total, width), jnp.bfloat16)
    narrow = jax.ShapeDtypeStruct((total, hidden), jnp.bfloat16)
    return pl.pallas_call(
        functools.partial(forward_kernel, len(pairs)),
        grid=(pl.cdiv(hidden, tile),),
        in_specs=specs
        + [
            pl.BlockSpec((width, tile), lambda j: (0, j)),
            pl.BlockSpec((tile, width), lambda j: (j, 0)),
        ],
        out_specs=[pl.BlockSpec((total, width), lambda j: (0, 0), pipeline_mode=once)] * 2
        + [pl.BlockSpec((total, tile), lambda j: (0, j))] * 2,
        out_shape=[whole, whole, narrow, narrow],
        compiler_params=pltpu.CompilerParams(vmem_limit_bytes=20 * 1024 * 1024),
        cost_estimate=pl.CostEstimate(
            flops=4 * total * width * hidden,
            bytes_accessed=4 * width * hidden + 8 * total * width + 4 * total * hidden,
            transcendentals=total * hidden,
        ),
    )(*operands, first_b, second_b)


def add(left, right):
    return (left.astype(jnp.float32) + right.astype(jnp.float32)).astype(jnp.bfloat16)


def halves(block, bit, axis=0):
    size = block.shape[axis] // 2
    kept = lax.dynamic_slice_in_dim(block, bit * size, size, axis)
    sent = lax.dynamic_slice_in_dim(block, (1 - bit) * size, size, axis)
    return kept, sent


def place(whole, block, bit, start=0):
    return lax.dynamic_update_slice_in_dim(whole, block, start + bit * block.shape[0], 0)


def shards(tokens, cotangent, w_one, w_two, late_two, round_index):
    first_b = w_one[0]
    second_b = w_two[0]
    path_rows = tokens.shape[3] * lax.axis_size("shard")
    step_rate = inner_rate / math.sqrt(path_rows)
    row = lax.axis_index("row")
    low_bit = ((row + 1) // 2) % 2
    high_bit = row // 2
    core_bit = lax.axis_index("col") % 2
    cols = lax.axis_size("col")
    rows = lax.axis_size("row")
    outer_rate = (
        0.7 * jnp.minimum(round_index + 1, warm_rounds).astype(jnp.float32) / float(warm_rounds)
    )

    state = {}
    for step in range(2):
        state["%do" % step] = jnp.concatenate([tokens[0, 0, step], cotangent[0, 0, step]], axis=1)
    width = tokens.shape[4]
    state["w1"], state["w2"] = first_b, second_b

    def rest_of_block(tag, kind):
        return state[tag][:, :width] if kind == "x" else state[tag][:, width:]

    def ahead(step, ends, tag):
        blocks = [state[str(step) + e] for e in ends.split()]
        pairs = [((e, 0), (e, 1)) for e in blocks]
        values = forward(pairs, state["w1"], state["w2"])
        state.update(zip(("n" + tag, "g" + tag, "u" + tag, "q" + tag), values))

    def ahead_last(step, tag):
        pairs = [((state["%dex" % step], 0), (state["%deg" % step], 0))]
        values = forward(pairs, state["w1"], state["w2"])
        state.update(zip(("n" + tag, "g" + tag, "u" + tag, "q" + tag), values))

    def grad_one(tags):
        n, q = [jnp.concatenate([state[k + t] for t in tags.split()]) for k in "nq"]
        grad = jnp.dot(n.T, q, preferred_element_type=jnp.float32) * D ** (-0.5)
        return step_rate * grad

    def grad_two(tags):
        u, g = [jnp.concatenate([state[k + t] for t in tags.split()]) for k in "ug"]
        grad = jnp.dot(u.T, g, preferred_element_type=jnp.float32) * FF ** (-0.5)
        return step_rate * grad

    def grow(name, grad):
        state[name] = (state[name].astype(jnp.float32) + grad).astype(jnp.bfloat16)

    def first_moves(step):
        own = "%do" % step
        for end, way in (("b", "up"), ("a", "down"), ("s", "side")):
            state[str(step) + end] = move(state[own], way, "gather_%d%s" % (step, end))

    def second_moves(step):
        for end, sent, way in (("f", "b", "up"), ("c", "s", "down"), ("d", "b", "side")):
            state[str(step) + end] = move(
                state[str(step) + sent], way, "gather_%d%s" % (step, end)
            )

    def last_moves(step):
        low = move(rest_of_block("%dd" % step, "x"), "up", "gather_%dex" % step)
        high = move(rest_of_block("%dc" % step, "g"), "down", "gather_%deg" % step)
        state["%dex" % step], state["%deg" % step] = low, high

    first_moves(0)
    state["new"] = (
        second_b.astype(jnp.float32) - outer_rate * late_two[0].astype(jnp.float32)
    ).astype(jnp.bfloat16)
    tie(state, "0b 0a 0s 0o 1o new")
    second_moves(0)
    ahead(0, "o b a s", "0n")
    state["1o"] = after(state["1o"], state["q0n"])
    state["1b"] = move(state["1o"], "up", "gather_1b")
    state["1a"] = move(state["1o"], "down", "gather_1a")
    state["d1"] = grad_one("0n").astype(jnp.bfloat16)
    state["d2"] = grad_two("0n").astype(jnp.bfloat16)
    tie(state, "0f 0c 0d n0n g0n u0n q0n d1 d2 1o")
    last_moves(0)
    state["1s"] = move(state["1o"], "side", "gather_1s")
    ahead(0, "f c d", "0m")
    tie(state, "1b 1a 1s d1 d2 n0m g0m u0m q0m w1 w2")
    second_moves(1)
    ahead_last(0, "0l")
    grow("d1", grad_one("0m 0l")), grow("d2", grad_two("0m 0l"))
    tie(state, "d1 d2")
    state["w1"] = (first_b.astype(jnp.float32) - state["d1"].astype(jnp.float32)).astype(jnp.bfloat16)
    state["w2"] = (second_b.astype(jnp.float32) - state["d2"].astype(jnp.float32)).astype(jnp.bfloat16)
    tie(state, "d1 d2 w1 w2")
    ahead(1, "o b a s", "1n")
    tie(state, "1f 1c 1d n1n g1n u1n q1n d1 d2")
    last_moves(1)
    grow("d1", grad_one("1n")), grow("d2", grad_two("1n"))
    ahead(1, "f c d", "1m")
    tie(state, "1ex 1eg n1m g1m u1m q1m d1 d2")
    ahead_last(1, "1l")

    def part(array, bit, parts, axis):
        size = array.shape[axis] // parts
        return lax.dynamic_slice_in_dim(array, bit * size, size, axis)

    def delta_one(bit):
        n, q = [jnp.concatenate([state[k + t] for t in ("1m", "1l")]) for k in "nq"]
        n = part(n, bit, 2, 1)
        grad = jnp.dot(n.T, q, preferred_element_type=jnp.float32) * D ** (-0.5)
        old = part(state["d1"], bit, 2, 0).astype(jnp.float32)
        return (old + step_rate * grad).astype(jnp.bfloat16)

    def delta_two(quarter):
        u, g = [jnp.concatenate([state[k + t] for t in ("1m", "1l")]) for k in "ug"]
        g = part(g, quarter, 4, 1)
        grad = jnp.dot(u.T, g, preferred_element_type=jnp.float32) * FF ** (-0.5)
        old = part(state["d2"], quarter, 4, 1).astype(jnp.float32)
        return (old + step_rate * grad).astype(jnp.bfloat16)

    ways = {
        "a": (even_pairs, odd_pairs, low_bit, high_bit, 0),
        "b": (odd_pairs, even_pairs, high_bit, low_bit, 2),
    }

    def trade(block, pairs, name):
        with jax.named_scope(name):
            return lax.ppermute(block, "row", pairs)

    state["s1"] = delta_one(1 - core_bit)
    with jax.named_scope("col_1"):
        other_one = lax.ppermute(state["s1"], "col", across_core)
    tie(state, "s1 u1m u1l g1m g1l d2")
    got, kept = {}, {}
    for p, (first, second, first_bit, second_bit, start) in ways.items():
        state["s" + p] = delta_two(start + 1 - first_bit)
        got[p] = trade(state["s" + p], first, "row_1" + p)
    tie(state, "sa sb n1m n1l q1m q1l d1 u1m u1l g1m g1l d2")
    total_one = add(delta_one(core_bit), other_one)
    with jax.named_scope("col_2"):
        other_one = lax.ppermute(total_one, "col", across_half)
    for p, (first, second, first_bit, second_bit, start) in ways.items():
        kept[p] = delta_two(start + first_bit)

    rows_two = second_b.shape[0]
    half = rows_two // 2
    fresh = {}
    for c in range(2):
        chunk = slice(c * half, (c + 1) * half)
        for p, (first, second, first_bit, second_bit, start) in ways.items():
            total = add(kept[p][chunk], after(got[p], total_one)[chunk])
            keep, sent = halves(total, second_bit, 1)
            other = trade(sent, second, "row_2%s%d" % (p, c))
            total = keep.astype(jnp.float32) + other.astype(jnp.float32)
            mine = (total / rows).astype(jnp.bfloat16)
            theirs = trade(mine, second, "row_3%s%d" % (p, c))
            size = mine.shape[1]
            mine, theirs = [
                jnp.where(second_bit == 0, l, r) for l, r in ((mine, theirs), (theirs, mine))
            ]
            mine = jnp.concatenate([mine, theirs], axis=1)
            fresh[p, c] = mine, trade(mine, first, "row_4%s%d" % (p, c))

    last = fresh["b", 1][0]
    mean_one = (
        total_one.astype(jnp.float32) + after(other_one, last).astype(jnp.float32)
    ) / cols
    half_rows = first_b.shape[0] // 2
    own_first = lax.dynamic_slice_in_dim(first_b, core_bit * half_rows, half_rows, 0)
    mine_one = (own_first.astype(jnp.float32) - outer_rate * mean_one).astype(jnp.bfloat16)
    with jax.named_scope("col_3"):
        theirs_one = lax.ppermute(mine_one, "col", across_core)

    new_one = place(jnp.zeros(first_b.shape, jnp.bfloat16), mine_one, core_bit)
    new_one = place(new_one, theirs_one, 1 - core_bit)
    fresh_two = jnp.zeros(second_b.shape, jnp.bfloat16)
    for (p, c), (mine, theirs) in fresh.items():
        first_bit, start, size = ways[p][2], ways[p][4], mine.shape[1]
        if (p, c) == ("b", 1):
            theirs, new_one = lax.optimization_barrier((theirs, new_one))
        fresh_two = lax.dynamic_update_slice(
            fresh_two, mine, (c * half, (start + first_bit) * size)
        )
        fresh_two = lax.dynamic_update_slice(
            fresh_two, theirs, (c * half, (start + 1 - first_bit) * size)
        )
    return (new_one[None], state["new"][None], fresh_two[None])


def solution(mesh):
    in_specs = (
        P("row", "col", None, "shard", None),
        P("row", "col", None, "shard", None),
        P("row", None, "shard"),
        P("col", "shard", None),
        P("col", "shard", None),
        P(),
    )
    out_specs = (P("row", None, "shard"), P("col", "shard", None), P("col", "shard", None))
    return jax.shard_map(shards, mesh=mesh, in_specs=in_specs, out_specs=out_specs, check_vma=False)
```
